32 devices in a mesh: groups: 2 (over y), chan: 4 (over z), win: 2 (over x), lag: 2 (over core).
Axes of the slice: x: 2, y: 2, z: 4, core: 2. Of those that a mesh axis runs over, the one named last changes fastest.
Arguments:
- spectra: bfloat16 [32, 2, 256, 1024], P('win', None, ('groups', 'chan'), 'lag'), parts along dimension 2, may hold values from -6 to 6
- dead_mask: int32 [256], P(('groups', 'chan')), parts along dimension 0, may hold values 0 or 1
- partners: int32 [4, 4], replicated, may hold values from -1 to 3, as said below
Outputs:
- correlations: float32 [256, 4, 32, 512], P(('groups', 'chan'), None, 'win', 'lag'), parts along dimension 0
The draws below stay inside these ranges and needn't reach their ends.
There are 2 independent parts, one for each index of `groups`. The reference program is written for one: setup_inputs(seed, part) draws one part's arguments, and reference() takes and returns one part's arrays. A program takes and returns all parts, laid end to end along the dimension named above; an argument that names none is the same for every part. Nothing has to cross between parts.
Inputs may be any that keep to these rules, and one draw needn't show every extreme that they name: `partners`: row p lists the blocks p, p + 1, ... up to p + r - 1, where the reach r of 1 to 4 is drawn for each row and is 4 in row 0; blocks past the last and slots past the reach hold -1.
All inputs are finite; a program needn't handle non-finite values. No bound on the sum of `dead_mask` on one device may be relied on, other than what follows from the above.
Results may differ from the reference program's by a relative error of at most 0.0024.
Values may be sent and summed in bfloat16 or wider, within the bound.
A program may use at most 192 MiB of HBM per device.

```python
import math
import jax
import jax.numpy as jnp
from jax import lax

CB = 32
F = 1024
LAGS = 512
BAND = 3
NSAMP = 15000
FLOW = 60
W = 32
C = 128
NB = 4


def draw_partners(key, part):
    reach = jax.random.randint(jax.random.fold_in(key, 7), (NB, 1), 1, BAND + 2)
    rows = jnp.arange(NB, dtype=jnp.int32)[:, None]
    reach = jnp.where(rows == 0, BAND + 1, reach)
    slots = jnp.arange(BAND + 1, dtype=jnp.int32)[None, :]
    target = rows + slots
    keep = (slots < reach) & (target < NB)
    return jnp.where(keep, target, -1).astype(jnp.int32)


def plant(values, own_key, low, high):
    spot = [jax.random.randint(jax.random.fold_in(own_key, axis), (), 0, length) for axis, length in enumerate(values.shape)]
    widest = values.shape.index(max(values.shape))
    neighbour = spot[:widest] + [(spot[widest] + 1) % values.shape[widest]] + spot[widest + 1:]
    return values.at[tuple(spot)].set(low).at[tuple(neighbour)].set(high)


def levels(own_key, dims, cuts, low, high):
    loudness = 1.0
    for position, parts in cuts:
        draws = jax.random.uniform(jax.random.fold_in(jax.random.fold_in(own_key, 6), position), (parts,), jnp.float32, low / len(cuts), high / len(cuts))
        loudness = loudness * jnp.repeat(jnp.exp(draws), dims[position] // parts).reshape((-1,) + (1,) * (len(dims) - 1 - position))
    return loudness


def noise(own_key, extent, scale, most, pieces=(), kind=jnp.bfloat16):
    drawn = jax.random.normal(own_key, extent, jnp.float32) * scale
    if len(pieces) > 0:
        drawn = levels(own_key, extent, pieces, -0.22, 0.18) * drawn
    return jnp.clip(drawn, min=-most, max=most).astype(kind)


def setup_inputs(seed: int = 0, part: int = 0) -> dict:
    key_list = jax.random.split(jax.random.key(seed), 4)
    part_keys = jax.random.split(jax.random.fold_in(key_list[3], part), 4)
    return {
        "spectra": noise(part_keys[0], (W, 2, C, F), 1.0, 6.0, ((0, 2), (2, 4), (3, 2))),
        "dead_mask": plant((jax.random.randint(part_keys[1], (C,), 0, 16) < 15).astype(jnp.int32), jax.random.fold_in(part_keys[1], 1), 0, 1),
        "partners": draw_partners(jax.random.fold_in(key_list[3], 71), part),
    }


water_level = 0.5

def whiten(spectra, dead_mask):
    values = spectra.astype(jnp.float32)
    amplitude = jnp.sqrt(values[:, 0] * values[:, 0] + values[:, 1] * values[:, 1])
    factor = dead_mask.astype(jnp.float32)[None, :, None] / jnp.maximum(amplitude, water_level)
    return (values * factor[:, None]).astype(jnp.bfloat16)

def phase_table(first_bin, bin_count):
    bins = FLOW + first_bin + jnp.arange(bin_count, dtype=jnp.int32)
    offsets = jnp.arange(LAGS, dtype=jnp.int32) - LAGS // 2
    turns = jnp.mod(bins[:, None] * offsets[None, :], NSAMP)
    angle = turns.astype(jnp.float32) * (2.0 * math.pi / NSAMP)
    return jnp.concatenate([jnp.cos(angle), -jnp.sin(angle)], axis=0)

def cross_spectra(own_block, partner):
    own_block = own_block.astype(jnp.float32)
    partner = partner.astype(jnp.float32)

    def product(left, right):
        return jnp.einsum('waf,kwjf->akjf', left, right, precision=lax.Precision.HIGHEST)
    real_part = product(own_block[:, 0], partner[:, :, 0]) + product(own_block[:, 1], partner[:, :, 1])
    imag_part = product(own_block[:, 1], partner[:, :, 0]) - product(own_block[:, 0], partner[:, :, 1])
    return jnp.stack([real_part, imag_part], axis=3)

def transform(stacked, table):
    shape = stacked.shape
    flat = stacked.reshape(shape[0] * shape[1] * shape[2], shape[3] * shape[4])
    result = jnp.dot(flat, table, precision=lax.Precision.HIGHEST, preferred_element_type=jnp.float32)
    return result.reshape(shape[0], shape[1], shape[2], table.shape[1])

def reference(spectra, dead_mask, partners):
    whitened = whiten(spectra, dead_mask)
    table = phase_table(jnp.int32(0), F)
    scale = (W * F) ** (-0.5)

    def one_block(block):
        own_block = lax.dynamic_slice_in_dim(whitened, (block * CB).astype(jnp.int32), CB, 2)
        targets = partners[block]

        def pick_block(target):
            first_row = (jnp.maximum(target, 0) * CB).astype(jnp.int32)
            piece = lax.dynamic_slice_in_dim(whitened, first_row, CB, 2)
            return jnp.where(target >= 0, piece, jnp.zeros_like(piece))
        partner = jax.vmap(pick_block)(targets)
        stacked = cross_spectra(own_block, partner)
        return transform(stacked, table) * scale
    blocks = lax.map(one_block, jnp.arange(NB, dtype=jnp.int32))
    return blocks.reshape(C, BAND + 1, CB, LAGS)
```

```python
import functools
import math

import jax
import jax.numpy as jnp
from jax import lax
from jax.experimental import pallas as pl
from jax.experimental.pallas import tpu as pltpu
from jax.sharding import PartitionSpec as P

LAGS = 512
NSAMP = 15000
FLOW = 60
LANES = 128
ROWS_AT_ONCE = 4

water_level = 0.5

MESH = pl.DeviceIdType.MESH
F32 = jnp.float32
BF16 = jnp.bfloat16


def kernel(
    sizes, spectra, mask, out, own, ybuf, xf, yf, pacc, cos_hi, cos_lo, sin_hi, sin_lo,
    outgoing, incoming, xs, xr, zs, zr, ls, lr,
):
    blocks, win, slots = sizes
    w_here, _, chans, bins = spectra.shape
    share = chans // win
    half = LAGS // 2
    c = lax.axis_index("chan")
    w = lax.axis_index("win")
    lag = lax.axis_index("lag")
    scale = (w_here * win * bins * 2) ** (-0.5)

    def lag_copy(k):
        return pltpu.make_async_remote_copy(
            outgoing.at[k], incoming.at[k], ls.at[k], lr.at[k],
            device_id={"lag": 1 - lag}, device_id_type=MESH)

    def win_send(d, n):
        peer = lax.rem(w + d, win)
        g = lax.rem(peer + n, win)
        return pltpu.make_async_remote_copy(
            own.at[w, g], own.at[w, g], xs.at[d - 1, n], xr.at[d - 1, n],
            device_id={"win": peer}, device_id_type=MESH)

    def win_arrival(d, n):
        source = lax.rem(w + win - d, win)
        g = lax.rem(w + n, win)
        return pltpu.make_async_remote_copy(
            own.at[source, g], own.at[source, g], xs.at[d - 1, n], xr.at[d - 1, n],
            device_id={"win": source}, device_id_type=MESH)

    def down(k, i):
        g = lax.rem(w + i, win)
        src = own.at[g, w] if k == 1 else ybuf.at[k - 2, i]
        return pltpu.make_async_remote_copy(
            src, ybuf.at[k - 1, i], zs.at[k - 1, i], zr.at[k - 1, i],
            device_id={"chan": c - 1}, device_id_type=MESH)

    def send_down(k, i):
        @pl.when((c >= 1) & (c + k - 1 < blocks))
        def _():
            down(k, i).start()

    barrier = pltpu.get_barrier_semaphore()
    pl.semaphore_signal(barrier, inc=1, device_id={"lag": 1 - lag}, device_id_type=MESH)
    for d in range(1, win):
        pl.semaphore_signal(barrier, inc=1, device_id={"win": lax.rem(w + d, win)}, device_id_type=MESH)

    @pl.when(c >= 1)
    def _():
        pl.semaphore_signal(barrier, inc=1, device_id={"chan": c - 1}, device_id_type=MESH)

    @pl.when(c + 1 < blocks)
    def _():
        pl.semaphore_signal(barrier, inc=1, device_id={"chan": c + 1}, device_id_type=MESH)

    def whiten(v, carry):
        re = spectra[v, 0].astype(F32)
        im = spectra[v, 1].astype(F32)
        amplitude = jnp.sqrt(re * re + im * im)
        factor = mask[:, 0:1] / jnp.maximum(amplitude, water_level)
        re = re * factor
        im = im * factor
        for g in range(win):
            rows = slice(g * share, (g + 1) * share)
            own[w, g, v] = jnp.concatenate([re[rows], im[rows]], axis=0).astype(BF16)
        return carry

    lax.fori_loop(0, w_here, whiten, 0)

    edges = (c >= 1).astype(jnp.int32) + (c + 1 < blocks).astype(jnp.int32)
    pl.semaphore_wait(barrier, win + edges)

    for d in range(1, win):
        win_send(d, 0).start()
    send_down(1, 0)
    for d in range(1, win):
        for n in range(1, win):
            win_send(d, n).start()

    def widen(group):
        def step(v, carry):
            for g in range(win):
                value = own[group, g, v].astype(F32)
                re, im = value[:share], value[share:]
                at = group * w_here + v
                for b in range(share // ROWS_AT_ONCE):
                    to = g * share // ROWS_AT_ONCE + b
                    rows = slice(b * ROWS_AT_ONCE, (b + 1) * ROWS_AT_ONCE)
                    for t, part in enumerate((re, im, re + im)):
                        xf[at, to, t * ROWS_AT_ONCE:(t + 1) * ROWS_AT_ONCE] = part[rows]
            return carry

        lax.fori_loop(0, w_here, step, 0)

    def stack_step(src, group, first):
        def convert(v, carry):
            value = src[v].astype(F32)
            re, im = value[:share], value[share:]
            yf[v, 0:share] = re
            yf[v, share:2 * share] = im
            yf[v, 2 * share:3 * share] = re - im
            return carry

        lax.fori_loop(0, w_here, convert, 0)
        tiles = bins // LANES

        def rows(n, carry):
            b = n // tiles
            a0 = b * ROWS_AT_ONCE
            col = pl.ds(pl.multiple_of(lax.rem(n, tiles) * LANES, LANES), LANES)
            total = [[None] * 3 for _ in range(ROWS_AT_ONCE)]
            for aa in range(ROWS_AT_ONCE):
                for t in range(3):
                    if first:
                        total[aa][t] = jnp.zeros((share, LANES), F32)
                    else:
                        total[aa][t] = pacc[t, pl.ds(pl.multiple_of((a0 + aa) * share, share), share), col]
            for v in range(w_here):
                y = [yf[v, t * share:(t + 1) * share, col] for t in range(3)]
                for aa in range(ROWS_AT_ONCE):
                    for t in range(3):
                        line = t * ROWS_AT_ONCE + aa
                        x = xf[group * w_here + v, b, line:line + 1, col]
                        total[aa][t] = total[aa][t] + x * y[t]
            for aa in range(ROWS_AT_ONCE):
                for t in range(3):
                    pacc[t, pl.ds(pl.multiple_of((a0 + aa) * share, share), share), col] = total[aa][t]
            return carry

        lax.fori_loop(0, (chans // ROWS_AT_ONCE) * tiles, rows, 0)

    at_once = 256 // share
    parts = chans // at_once

    def transform(k):
        def part(n, carry):
            r = pl.ds(pl.multiple_of(n * 256, 256), 256)
            p1, p2, p3 = pacc[0, r], pacc[1, r], pacc[2, r]
            re = p1 + p2
            im = p3 - p1 + p2
            re_hi = re.astype(BF16)
            re_lo = (re - re_hi.astype(F32)).astype(BF16)
            im_hi = im.astype(BF16)
            im_lo = (im - im_hi.astype(F32)).astype(BF16)
            dot = functools.partial(jnp.dot, preferred_element_type=F32)
            total = dot(re_hi, cos_hi[...]) + dot(im_hi, sin_hi[...])
            total += dot(re_lo, cos_hi[...]) + dot(im_lo, sin_hi[...])
            total += dot(re_hi, cos_lo[...]) + dot(im_hi, sin_lo[...])
            here = total[:, :half].reshape(at_once, share, half)
            there = total[:, half:].reshape(at_once, share, half)
            a = pl.ds(n * at_once, at_once)
            out[a, k] = here
            outgoing[k, a] = there
            return carry

        lax.fori_loop(0, parts, part, 0)
        lag_copy(k).start()

    def settle(k):
        lag_copy(k).wait()

        def add(n, carry):
            a = pl.ds(n * 4, 4)
            out[a, k] = (out[a, k] + incoming[k, a]) * scale
            return carry

        lax.fori_loop(0, chans // 4, add, 0)

    def phases(n, carry):
        r = pl.ds(pl.multiple_of(n * 16, 16), 16)
        bin_no = FLOW + lag * bins + n * 16 + lax.broadcasted_iota(jnp.int32, (16, LAGS), 0)
        place = lax.broadcasted_iota(jnp.int32, (16, LAGS), 1) + lag * half
        place = jnp.where(place >= LAGS, place - LAGS, place) - LAGS // 2
        product = bin_no * place
        laps = jnp.floor(product.astype(F32) * (1.0 / NSAMP)).astype(jnp.int32)
        turns = product - laps * NSAMP
        turns = jnp.where(turns < 0, turns + NSAMP, turns)
        turns = jnp.where(turns >= NSAMP, turns - NSAMP, turns)
        angle = turns.astype(F32) * (2.0 * math.pi / NSAMP)
        cos, sin = jnp.cos(angle), -jnp.sin(angle)
        hi = cos.astype(BF16)
        cos_hi[r] = hi
        cos_lo[r] = (cos - hi.astype(F32)).astype(BF16)
        hi = sin.astype(BF16)
        sin_hi[r] = hi
        sin_lo[r] = (sin - hi.astype(F32)).astype(BF16)
        return carry

    lax.fori_loop(0, bins // 16, phases, 0)

    widen(w)
    stack_step(own.at[w, w], w, True)
    for i in range(1, win):
        d = win - i
        win_arrival(d, 0).wait_recv()
        send_down(1, i)
        for n in range(1, win):
            win_arrival(d, n).wait_recv()
        group = lax.rem(w + i, win)
        widen(group)
        stack_step(own.at[group, w], group, False)
    transform(0)

    for k in range(1, slots):
        have = c + k < blocks

        @pl.when(have)
        def _(k=k):
            for i in range(win):
                down(k, i).wait_recv()
                if k + 1 < slots:
                    send_down(k + 1, i)
                stack_step(ybuf.at[k - 1, i], lax.rem(w + i, win), i == 0)
                if i == 0 and k == 1:
                    settle(0)
            if k > 1:
                settle(k - 1)
            transform(k)

        @pl.when(jnp.logical_not(have))
        def _(k=k):
            out[:, k] = jnp.zeros((chans, share, half), F32)

    for k in range(slots):
        last = (c + k < blocks) if k == slots - 1 else (c + k == blocks - 1)

        @pl.when(last)
        def _(k=k):
            settle(k)

    for k in range(1, slots):
        @pl.when((c >= 1) & (c + k - 1 < blocks))
        def _(k=k):
            for i in range(win):
                down(k, i).wait_send()

    for d in range(1, win):
        for n in range(win):
            win_send(d, n).wait_send()


def body(blocks, win, spectra, dead_mask, partners):
    w_here, _, chans, bins = spectra.shape
    slots = partners.shape[1]
    share = chans // win
    half = LAGS // 2
    mask = jnp.broadcast_to(dead_mask.astype(F32)[:, None], (chans, LANES))
    dma = pltpu.SemaphoreType.DMA
    raw = pl.pallas_call(
        functools.partial(kernel, (blocks, win, slots)),
        out_shape=jax.ShapeDtypeStruct((chans, slots, share, half), F32),
        in_specs=[pl.BlockSpec(memory_space=pltpu.VMEM)] * 2,
        out_specs=pl.BlockSpec(memory_space=pltpu.VMEM),
        scratch_shapes=[
            pltpu.VMEM((win, win, w_here, 2 * share, bins), BF16),
            pltpu.VMEM((slots - 1, win, w_here, 2 * share, bins), BF16),
            pltpu.VMEM((win * w_here, chans // ROWS_AT_ONCE, 4 * ROWS_AT_ONCE, bins), F32),
            pltpu.VMEM((w_here, 3 * share, bins), F32),
            pltpu.VMEM((3, chans * share, bins), F32),
            pltpu.VMEM((bins, LAGS), BF16),
            pltpu.VMEM((bins, LAGS), BF16),
            pltpu.VMEM((bins, LAGS), BF16),
            pltpu.VMEM((bins, LAGS), BF16),
            pltpu.VMEM((slots, chans, share, half), F32),
            pltpu.VMEM((slots, chans, share, half), F32),
            dma((win - 1, win)),
            dma((win - 1, win)),
            dma((slots - 1, win)),
            dma((slots - 1, win)),
            dma((slots,)),
            dma((slots,)),
        ],
        compiler_params=pltpu.CompilerParams(
            collective_id=0, has_side_effects=True, vmem_limit_bytes=50 * 2**20),
    )(spectra, mask)
    wanted = lax.dynamic_index_in_dim(partners, lax.axis_index("chan"), 0, keepdims=False)
    return jnp.where(wanted[None, :, None, None] >= 0, raw, 0.0)


def solution(mesh):
    placed = (P("win", None, ("groups", "chan"), "lag"), P(("groups", "chan")), P())
    return jax.shard_map(
        functools.partial(body, mesh.shape["chan"], mesh.shape["win"]),
        mesh=mesh,
        in_specs=placed,
        out_specs=P(("groups", "chan"), None, "win", "lag"),
        check_vma=False,
    )
```

```python
import functools
import math

import jax
import jax.numpy as jnp
from jax import lax
from jax.experimental import pallas as pl
from jax.experimental.pallas import tpu as pltpu
from jax.sharding import PartitionSpec as P

LAGS = 512
NSAMP = 15000
FLOW = 60
LANES = 128
ROWS_AT_ONCE = 4

water_level = 0.5

MESH = pl.DeviceIdType.MESH
F32 = jnp.float32
BF16 = jnp.bfloat16


def kernel(
    sizes, spectra, mask, out, own, ybuf, below, got, xf, yf, pacc, cos_hi, cos_lo, sin_hi, sin_lo,
    outgoing, incoming, xs, xr, zs, zr, us, ur, rs, rr, ls, lr, fs, fr,
):
    blocks, win, slots = sizes
    w_here, _, chans, bins = spectra.shape
    share = chans // win
    half = LAGS // 2
    c = lax.axis_index("chan")
    w = lax.axis_index("win")
    lag = lax.axis_index("lag")
    scale = (w_here * win * bins * 2) ** (-0.5)

    def lag_copy(k):
        return pltpu.make_async_remote_copy(
            outgoing.at[k], incoming.at[k], ls.at[k], lr.at[k],
            device_id={"lag": 1 - lag}, device_id_type=MESH)

    def win_send(d, n):
        peer = lax.rem(w + d, win)
        g = lax.rem(peer + n, win)
        return pltpu.make_async_remote_copy(
            own.at[w, g], own.at[w, g], xs.at[d - 1, n], xr.at[d - 1, n],
            device_id={"win": peer}, device_id_type=MESH)

    def win_arrival(d, n):
        source = lax.rem(w + win - d, win)
        g = lax.rem(w + n, win)
        return pltpu.make_async_remote_copy(
            own.at[source, g], own.at[source, g], xs.at[d - 1, n], xr.at[d - 1, n],
            device_id={"win": source}, device_id_type=MESH)

    def down(k, i):
        g = lax.rem(w + i, win)
        src = own.at[g, w] if k == 1 else ybuf.at[k - 2, i]
        return pltpu.make_async_remote_copy(
            src, ybuf.at[k - 1, i], zs.at[k - 1, i], zr.at[k - 1, i],
            device_id={"chan": c - 1}, device_id_type=MESH)

    far = slots - 1
    gives = c + far < blocks
    takes = (c >= 1) & (c - 1 + far < blocks)
    at_once = 256 // share
    parts = chans // at_once

    def up(i):
        g = lax.rem(w + i, win)
        return pltpu.make_async_remote_copy(
            own.at[g], below.at[g], us.at[i], ur.at[i],
            device_id={"chan": c + 1}, device_id_type=MESH)

    def far_lag(n):
        a = pl.ds(n * at_once, at_once)
        return pltpu.make_async_remote_copy(
            outgoing.at[far, a], incoming.at[far, a], fs.at[n], fr.at[n],
            device_id={"lag": 1 - lag}, device_id_type=MESH)

    def far_result(n):
        a = pl.ds(n * at_once, at_once)
        return pltpu.make_async_remote_copy(
            got.at[0, a], got.at[1, a], rs.at[n], rr.at[n],
            device_id={"chan": c - 1}, device_id_type=MESH)

    def send_up(i):
        @pl.when(gives)
        def _():
            up(i).start()

    def send_down(k, i):
        @pl.when((c >= 1) & (c + k - 1 < blocks))
        def _():
            down(k, i).start()

    barrier = pltpu.get_barrier_semaphore()
    pl.semaphore_signal(barrier, inc=1, device_id={"lag": 1 - lag}, device_id_type=MESH)
    for d in range(1, win):
        pl.semaphore_signal(barrier, inc=1, device_id={"win": lax.rem(w + d, win)}, device_id_type=MESH)

    @pl.when(c >= 1)
    def _():
        pl.semaphore_signal(barrier, inc=1, device_id={"chan": c - 1}, device_id_type=MESH)

    @pl.when(c + 1 < blocks)
    def _():
        pl.semaphore_signal(barrier, inc=1, device_id={"chan": c + 1}, device_id_type=MESH)

    def whiten(v, carry):
        re = spectra[v, 0].astype(F32)
        im = spectra[v, 1].astype(F32)
        amplitude = jnp.sqrt(re * re + im * im)
        factor = mask[:, 0:1] / jnp.maximum(amplitude, water_level)
        re = re * factor
        im = im * factor
        for g in range(win):
            rows = slice(g * share, (g + 1) * share)
            own[w, g, v] = jnp.concatenate([re[rows], im[rows]], axis=0).astype(BF16)
        return carry

    lax.fori_loop(0, w_here, whiten, 0)

    edges = (c >= 1).astype(jnp.int32) + (c + 1 < blocks).astype(jnp.int32)
    pl.semaphore_wait(barrier, win + edges)

    for d in range(1, win):
        win_send(d, 0).start()
    send_down(1, 0)
    send_up(0)
    for d in range(1, win):
        for n in range(1, win):
            win_send(d, n).start()

    def widen(blockref, group, which):
        def step(v, carry):
            for g in range(win):
                value = blockref[group, g, v].astype(F32)
                re, im = value[:share], value[share:]
                at = group * w_here + v
                for b in range(share // ROWS_AT_ONCE):
                    to = g * share // ROWS_AT_ONCE + b
                    rows = slice(b * ROWS_AT_ONCE, (b + 1) * ROWS_AT_ONCE)
                    for t, part in enumerate((re, im, re + im)):
                        xf[which, at, to, t * ROWS_AT_ONCE:(t + 1) * ROWS_AT_ONCE] = part[rows]
            return carry

        lax.fori_loop(0, w_here, step, 0)

    def stack_step(src, group, first, which=0):
        def convert(v, carry):
            value = src[v].astype(F32)
            re, im = value[:share], value[share:]
            yf[v, 0:share] = re
            yf[v, share:2 * share] = im
            yf[v, 2 * share:3 * share] = re - im
            return carry

        lax.fori_loop(0, w_here, convert, 0)
        tiles = bins // LANES

        def rows(n, carry):
            b = n // tiles
            a0 = b * ROWS_AT_ONCE
            col = pl.ds(pl.multiple_of(lax.rem(n, tiles) * LANES, LANES), LANES)
            total = [[None] * 3 for _ in range(ROWS_AT_ONCE)]
            for aa in range(ROWS_AT_ONCE):
                for t in range(3):
                    if first:
                        total[aa][t] = jnp.zeros((share, LANES), F32)
                    else:
                        total[aa][t] = pacc[which, t, pl.ds(pl.multiple_of((a0 + aa) * share, share), share), col]
            for v in range(w_here):
                y = [yf[v, t * share:(t + 1) * share, col] for t in range(3)]
                for aa in range(ROWS_AT_ONCE):
                    for t in range(3):
                        line = t * ROWS_AT_ONCE + aa
                        x = xf[which, group * w_here + v, b, line:line + 1, col]
                        total[aa][t] = total[aa][t] + x * y[t]
            for aa in range(ROWS_AT_ONCE):
                for t in range(3):
                    pacc[which, t, pl.ds(pl.multiple_of((a0 + aa) * share, share), share), col] = total[aa][t]
            return carry

        lax.fori_loop(0, (chans // ROWS_AT_ONCE) * tiles, rows, 0)

    def rows_out(n, which):
            r = pl.ds(pl.multiple_of(n * 256, 256), 256)
            p1, p2, p3 = pacc[which, 0, r], pacc[which, 1, r], pacc[which, 2, r]
            re = p1 + p2
            im = p3 - p1 + p2
            re_hi = re.astype(BF16)
            re_lo = (re - re_hi.astype(F32)).astype(BF16)
            im_hi = im.astype(BF16)
            im_lo = (im - im_hi.astype(F32)).astype(BF16)
            dot = functools.partial(jnp.dot, preferred_element_type=F32)
            total = dot(re_hi, cos_hi[...]) + dot(im_hi, sin_hi[...])
            total += dot(re_lo, cos_hi[...]) + dot(im_lo, sin_hi[...])
            total += dot(re_hi, cos_lo[...]) + dot(im_hi, sin_lo[...])
            here = total[:, :half].reshape(at_once, share, half)
            there = total[:, half:].reshape(at_once, share, half)
            return here, there

    def transform(k):
        def part(n, carry):
            a = pl.ds(n * at_once, at_once)
            out[a, k], outgoing[k, a] = rows_out(n, 0)
            return carry

        lax.fori_loop(0, parts, part, 0)
        lag_copy(k).start()

    def settle(k):
        lag_copy(k).wait()

        def add(n, carry):
            a = pl.ds(n * 4, 4)
            out[a, k] = (out[a, k] + incoming[k, a]) * scale
            return carry

        lax.fori_loop(0, chans // 4, add, 0)

    def phases(n, carry):
        r = pl.ds(pl.multiple_of(n * 16, 16), 16)
        bin_no = FLOW + lag * bins + n * 16 + lax.broadcasted_iota(jnp.int32, (16, LAGS), 0)
        place = lax.broadcasted_iota(jnp.int32, (16, LAGS), 1) + lag * half
        place = jnp.where(place >= LAGS, place - LAGS, place) - LAGS // 2
        product = bin_no * place
        laps = jnp.floor(product.astype(F32) * (1.0 / NSAMP)).astype(jnp.int32)
        turns = product - laps * NSAMP
        turns = jnp.where(turns < 0, turns + NSAMP, turns)
        turns = jnp.where(turns >= NSAMP, turns - NSAMP, turns)
        angle = turns.astype(F32) * (2.0 * math.pi / NSAMP)
        cos, sin = jnp.cos(angle), -jnp.sin(angle)
        hi = cos.astype(BF16)
        cos_hi[r] = hi
        cos_lo[r] = (cos - hi.astype(F32)).astype(BF16)
        hi = sin.astype(BF16)
        sin_hi[r] = hi
        sin_lo[r] = (sin - hi.astype(F32)).astype(BF16)
        return carry

    lax.fori_loop(0, bins // 16, phases, 0)

    def far_finish():
        for n in range(parts):
            a = pl.ds(n * at_once, at_once)
            got[0, a], outgoing[far, a] = rows_out(n, 1)
            far_lag(n).start()
        for n in range(parts):
            a = pl.ds(n * at_once, at_once)
            far_lag(n).wait()
            got[0, a] = (got[0, a] + incoming[far, a]) * scale
            far_result(n).start()

    widen(own, w, 0)
    stack_step(own.at[w, w], w, True)
    for i in range(1, win):
        d = win - i
        win_arrival(d, 0).wait_recv()
        send_down(1, i)
        for n in range(1, win):
            win_arrival(d, n).wait_recv()
        send_up(i)
        group = lax.rem(w + i, win)
        widen(own, group, 0)
        stack_step(own.at[group, w], group, False)
    transform(0)

    for k in range(1, far):
        have = c + k < blocks

        @pl.when(have)
        def _(k=k):
            for i in range(win):
                group = lax.rem(w + i, win)
                down(k, i).wait_recv()
                if k + 1 < far:
                    send_down(k + 1, i)
                else:
                    @pl.when(takes)
                    def _():
                        up(i).wait_recv()
                        widen(below, group, 1)
                        stack_step(ybuf.at[k - 1, i], group, i == 0, 1)
                        if i == win - 1:
                            far_finish()
                stack_step(ybuf.at[k - 1, i], group, i == 0)
                if i == 0:
                    settle(k - 1)
            transform(k)

        @pl.when(jnp.logical_not(have))
        def _(k=k):
            out[:, k] = jnp.zeros((chans, share, half), F32)

    for k in range(far):
        last = (c + k < blocks) if k == far - 1 else (c + k == blocks - 1)

        @pl.when(last)
        def _(k=k):
            settle(k)

    @pl.when(gives)
    def _():
        for n in range(parts):
            far_result(n).wait_recv()
            a = pl.ds(n * at_once, at_once)
            out[a, far] = got[1, a]
        for i in range(win):
            up(i).wait_send()

    @pl.when(jnp.logical_not(gives))
    def _():
        out[:, far] = jnp.zeros((chans, share, half), F32)

    @pl.when(takes)
    def _():
        for n in range(parts):
            far_result(n).wait_send()

    for k in range(1, far):
        @pl.when((c >= 1) & (c + k - 1 < blocks))
        def _(k=k):
            for i in range(win):
                down(k, i).wait_send()

    for d in range(1, win):
        for n in range(win):
            win_send(d, n).wait_send()


def body(blocks, win, spectra, dead_mask, partners):
    w_here, _, chans, bins = spectra.shape
    slots = partners.shape[1]
    share = chans // win
    half = LAGS // 2
    parts = chans * share // 256
    mask = jnp.broadcast_to(dead_mask.astype(F32)[:, None], (chans, LANES))
    dma = pltpu.SemaphoreType.DMA
    raw = pl.pallas_call(
        functools.partial(kernel, (blocks, win, slots)),
        out_shape=jax.ShapeDtypeStruct((chans, slots, share, half), F32),
        in_specs=[pl.BlockSpec(memory_space=pltpu.VMEM)] * 2,
        out_specs=pl.BlockSpec(memory_space=pltpu.VMEM),
        scratch_shapes=[
            pltpu.VMEM((win, win, w_here, 2 * share, bins), BF16),
            pltpu.VMEM((slots - 2, win, w_here, 2 * share, bins), BF16),
            pltpu.VMEM((win, win, w_here, 2 * share, bins), BF16),
            pltpu.VMEM((2, chans, share, half), F32),
            pltpu.VMEM((2, win * w_here, chans // ROWS_AT_ONCE, 4 * ROWS_AT_ONCE, bins), F32),
            pltpu.VMEM((w_here, 3 * share, bins), F32),
            pltpu.VMEM((2, 3, chans * share, bins), F32),
            pltpu.VMEM((bins, LAGS), BF16),
            pltpu.VMEM((bins, LAGS), BF16),
            pltpu.VMEM((bins, LAGS), BF16),
            pltpu.VMEM((bins, LAGS), BF16),
            pltpu.VMEM((slots, chans, share, half), F32),
            pltpu.VMEM((slots, chans, share, half), F32),
            dma((win - 1, win)),
            dma((win - 1, win)),
            dma((slots - 2, win)),
            dma((slots - 2, win)),
            dma((win,)),
            dma((win,)),
            dma((parts,)),
            dma((parts,)),
            dma((slots - 1,)),
            dma((slots - 1,)),
            dma((parts,)),
            dma((parts,)),
        ],
        compiler_params=pltpu.CompilerParams(
            collective_id=0, has_side_effects=True, vmem_limit_bytes=60 * 2**20),
    )(spectra, mask)
    wanted = lax.dynamic_index_in_dim(partners, lax.axis_index("chan"), 0, keepdims=False)
    return jnp.where(wanted[None, :, None, None] >= 0, raw, 0.0)


def solution(mesh):
    placed = (P("win", None, ("groups", "chan"), "lag"), P(("groups", "chan")), P())
    return jax.shard_map(
        functools.partial(body, mesh.shape["chan"], mesh.shape["win"]),
        mesh=mesh,
        in_specs=placed,
        out_specs=P(("groups", "chan"), None, "win", "lag"),
        check_vma=False,
    )
```

```python
import functools
import math

import jax
import jax.numpy as jnp
from jax import lax
from jax.experimental import pallas as pl
from jax.experimental.pallas import tpu as pltpu
from jax.sharding import PartitionSpec as P

LAGS = 512
NSAMP = 15000
FLOW = 60
LANES = 128
ROWS_AT_ONCE = 4
PIECES = 4

water_level = 0.5

MESH = pl.DeviceIdType.MESH
F32 = jnp.float32
BF16 = jnp.bfloat16


def kernel(
    sizes, spectra, mask, out, own, ybuf, below, got, xf, yf, pacc, cos_hi, cos_lo, sin_hi, sin_lo,
    outgoing, incoming, xs, xr, zs, zr, us, ur, rs, rr, ls, lr, fs, fr,
):
    blocks, win, slots = sizes
    w_here, _, chans, bins = spectra.shape
    share = chans // win
    half = LAGS // 2
    c = lax.axis_index("chan")
    w = lax.axis_index("win")
    lag = lax.axis_index("lag")
    scale = (w_here * win * bins * 2) ** (-0.5)

    def lag_copy(k):
        return pltpu.make_async_remote_copy(
            outgoing.at[k], incoming.at[k], ls.at[k], lr.at[k],
            device_id={"lag": 1 - lag}, device_id_type=MESH)

    def win_send(d, n):
        peer = lax.rem(w + d, win)
        g = lax.rem(peer + n, win)
        return pltpu.make_async_remote_copy(
            own.at[w, g], own.at[w, g], xs.at[d - 1, n], xr.at[d - 1, n],
            device_id={"win": peer}, device_id_type=MESH)

    def win_arrival(d, n):
        source = lax.rem(w + win - d, win)
        g = lax.rem(w + n, win)
        return pltpu.make_async_remote_copy(
            own.at[source, g], own.at[source, g], xs.at[d - 1, n], xr.at[d - 1, n],
            device_id={"win": source}, device_id_type=MESH)

    piece = w_here // PIECES

    def down(k, i, q):
        g = lax.rem(w + i, win)
        src = own.at[g, w] if k == 1 else ybuf.at[k - 2, i]
        part = pl.ds(q * piece, piece)
        return pltpu.make_async_remote_copy(
            src.at[part], ybuf.at[k - 1, i, part], zs.at[k - 1, i, q], zr.at[k - 1, i, q],
            device_id={"chan": c - 1}, device_id_type=MESH)

    far = slots - 1
    gives = c + far < blocks
    takes = (c >= 1) & (c - 1 + far < blocks)
    at_once = 256 // share
    parts = chans // at_once

    def up(i, q):
        g = lax.rem(w + i, win)
        part = pl.ds(q * piece, piece)
        return pltpu.make_async_remote_copy(
            own.at[g, :, part], below.at[g, :, part], us.at[i, q], ur.at[i, q],
            device_id={"chan": c + 1}, device_id_type=MESH)

    def far_lag(n):
        a = pl.ds(n * at_once, at_once)
        return pltpu.make_async_remote_copy(
            outgoing.at[far, a], incoming.at[far, a], fs.at[n], fr.at[n],
            device_id={"lag": 1 - lag}, device_id_type=MESH)

    def far_result(n):
        a = pl.ds(n * at_once, at_once)
        return pltpu.make_async_remote_copy(
            got.at[0, a], got.at[1, a], rs.at[n], rr.at[n],
            device_id={"chan": c - 1}, device_id_type=MESH)

    def send_up(i):
        @pl.when(gives)
        def _():
            for q in range(PIECES):
                up(i, q).start()

    def send_down(k, i):
        @pl.when((c >= 1) & (c + k - 1 < blocks))
        def _():
            for q in range(PIECES):
                down(k, i, q).start()

    barrier = pltpu.get_barrier_semaphore()
    pl.semaphore_signal(barrier, inc=1, device_id={"lag": 1 - lag}, device_id_type=MESH)
    for d in range(1, win):
        pl.semaphore_signal(barrier, inc=1, device_id={"win": lax.rem(w + d, win)}, device_id_type=MESH)

    @pl.when(c >= 1)
    def _():
        pl.semaphore_signal(barrier, inc=1, device_id={"chan": c - 1}, device_id_type=MESH)

    @pl.when(c + 1 < blocks)
    def _():
        pl.semaphore_signal(barrier, inc=1, device_id={"chan": c + 1}, device_id_type=MESH)

    def whiten(v, carry):
        re = spectra[v, 0].astype(F32)
        im = spectra[v, 1].astype(F32)
        amplitude = jnp.sqrt(re * re + im * im)
        factor = mask[:, 0:1] / jnp.maximum(amplitude, water_level)
        re = re * factor
        im = im * factor
        for g in range(win):
            rows = slice(g * share, (g + 1) * share)
            own[w, g, v] = jnp.concatenate([re[rows], im[rows]], axis=0).astype(BF16)
        return carry

    lax.fori_loop(0, w_here, whiten, 0)

    edges = (c >= 1).astype(jnp.int32) + (c + 1 < blocks).astype(jnp.int32)
    pl.semaphore_wait(barrier, win + edges)

    for d in range(1, win):
        win_send(d, 0).start()
    send_down(1, 0)
    send_up(0)
    for d in range(1, win):
        for n in range(1, win):
            win_send(d, n).start()

    def widen(blockref, group, which, start, count):
        def step(v, carry):
            for g in range(win):
                value = blockref[group, g, v].astype(F32)
                re, im = value[:share], value[share:]
                at = group * w_here + v
                for b in range(share // ROWS_AT_ONCE):
                    to = g * share // ROWS_AT_ONCE + b
                    rows = slice(b * ROWS_AT_ONCE, (b + 1) * ROWS_AT_ONCE)
                    for t, part in enumerate((re, im, re + im)):
                        xf[which, at, to, t * ROWS_AT_ONCE:(t + 1) * ROWS_AT_ONCE] = part[rows]
            return carry

        lax.fori_loop(start, start + count, step, 0)

    def stack_step(src, group, fresh, which, start, count):
        def convert(v, carry):
            value = src[start + v].astype(F32)
            re, im = value[:share], value[share:]
            yf[v, 0:share] = re
            yf[v, share:2 * share] = im
            yf[v, 2 * share:3 * share] = re - im
            return carry

        lax.fori_loop(0, count, convert, 0)
        tiles = bins // LANES

        def rows(n, carry):
            b = n // tiles
            a0 = b * ROWS_AT_ONCE
            col = pl.ds(pl.multiple_of(lax.rem(n, tiles) * LANES, LANES), LANES)
            total = [[None] * 3 for _ in range(ROWS_AT_ONCE)]
            for aa in range(ROWS_AT_ONCE):
                for t in range(3):
                    if fresh is True:
                        total[aa][t] = jnp.zeros((share, LANES), F32)
                    else:
                        total[aa][t] = pacc[which, t, pl.ds(pl.multiple_of((a0 + aa) * share, share), share), col]
                        if fresh is not False:
                            total[aa][t] = jnp.where(fresh, 0.0, total[aa][t])
            for v in range(count):
                y = [yf[v, t * share:(t + 1) * share, col] for t in range(3)]
                for aa in range(ROWS_AT_ONCE):
                    for t in range(3):
                        line = t * ROWS_AT_ONCE + aa
                        x = xf[which, group * w_here + start + v, b, line:line + 1, col]
                        total[aa][t] = total[aa][t] + x * y[t]
            for aa in range(ROWS_AT_ONCE):
                for t in range(3):
                    pacc[which, t, pl.ds(pl.multiple_of((a0 + aa) * share, share), share), col] = total[aa][t]
            return carry

        lax.fori_loop(0, (chans // ROWS_AT_ONCE) * tiles, rows, 0)

    def rows_out(n, which):
            r = pl.ds(pl.multiple_of(n * 256, 256), 256)
            p1, p2, p3 = pacc[which, 0, r], pacc[which, 1, r], pacc[which, 2, r]
            re = p1 + p2
            im = p3 - p1 + p2
            re_hi = re.astype(BF16)
            re_lo = (re - re_hi.astype(F32)).astype(BF16)
            im_hi = im.astype(BF16)
            im_lo = (im - im_hi.astype(F32)).astype(BF16)
            dot = functools.partial(jnp.dot, preferred_element_type=F32)
            total = dot(re_hi, cos_hi[...]) + dot(im_hi, sin_hi[...])
            total += dot(re_lo, cos_hi[...]) + dot(im_lo, sin_hi[...])
            total += dot(re_hi, cos_lo[...]) + dot(im_hi, sin_lo[...])
            here = total[:, :half].reshape(at_once, share, half)
            there = total[:, half:].reshape(at_once, share, half)
            return here, there

    def transform(k):
        def part(n, carry):
            a = pl.ds(n * at_once, at_once)
            out[a, k], outgoing[k, a] = rows_out(n, 0)
            return carry

        lax.fori_loop(0, parts, part, 0)
        lag_copy(k).start()

    def settle(k):
        lag_copy(k).wait()

        def add(n, carry):
            a = pl.ds(n * 4, 4)
            out[a, k] = (out[a, k] + incoming[k, a]) * scale
            return carry

        lax.fori_loop(0, chans // 4, add, 0)

    def phases(n, carry):
        r = pl.ds(pl.multiple_of(n * 16, 16), 16)
        bin_no = FLOW + lag * bins + n * 16 + lax.broadcasted_iota(jnp.int32, (16, LAGS), 0)
        place = lax.broadcasted_iota(jnp.int32, (16, LAGS), 1) + lag * half
        place = jnp.where(place >= LAGS, place - LAGS, place) - LAGS // 2
        product = bin_no * place
        laps = jnp.floor(product.astype(F32) * (1.0 / NSAMP)).astype(jnp.int32)
        turns = product - laps * NSAMP
        turns = jnp.where(turns < 0, turns + NSAMP, turns)
        turns = jnp.where(turns >= NSAMP, turns - NSAMP, turns)
        angle = turns.astype(F32) * (2.0 * math.pi / NSAMP)
        cos, sin = jnp.cos(angle), -jnp.sin(angle)
        hi = cos.astype(BF16)
        cos_hi[r] = hi
        cos_lo[r] = (cos - hi.astype(F32)).astype(BF16)
        hi = sin.astype(BF16)
        sin_hi[r] = hi
        sin_lo[r] = (sin - hi.astype(F32)).astype(BF16)
        return carry

    lax.fori_loop(0, bins // 16, phases, 0)

    def far_finish():
        for n in range(parts):
            a = pl.ds(n * at_once, at_once)
            got[0, a], outgoing[far, a] = rows_out(n, 1)
            far_lag(n).start()
        for n in range(parts):
            a = pl.ds(n * at_once, at_once)
            far_lag(n).wait()
            got[0, a] = (got[0, a] + incoming[far, a]) * scale
            far_result(n).start()

    def take(k, i):
        @pl.when(c + k < blocks)
        def _():
            for q in range(PIECES):
                down(k, i, q).wait_recv()
        send_down(k + 1, i)

    widen(own, w, 0, 0, w_here)
    stack_step(own.at[w, w], w, True, 0, 0, w_here)
    for i in range(1, win):
        d = win - i
        win_arrival(d, 0).wait_recv()
        send_down(1, i)
        for n in range(1, win):
            win_arrival(d, n).wait_recv()
        send_up(i)
        take(1, i - 1)
        group = lax.rem(w + i, win)
        widen(own, group, 0, 0, w_here)
        stack_step(own.at[group, w], group, False, 0, 0, w_here)
    take(1, win - 1)
    transform(0)

    def far_step(k, i, q):
        group = lax.rem(w + i, win)
        start = q * piece
        up(i, q).wait_recv()
        widen(below, group, 1, start, piece)
        stack_step(ybuf.at[k - 1, i], group, (q == 0) if i == 0 else False, 1, start, piece)

    for k in range(1, far):
        have = c + k < blocks

        @pl.when(have)
        def _(k=k):
            for i in range(win):
                group = lax.rem(w + i, win)
                if k + 1 == far:
                    def arrive(q, carry):
                        down(k, i, q).wait_recv()

                        @pl.when(takes)
                        def _():
                            far_step(k, i, q)
                        return carry

                    lax.fori_loop(0, PIECES, arrive, 0)
                    if i == win - 1:
                        pl.when(takes)(far_finish)
                elif k > 1:
                    take(k, i)
                stack_step(ybuf.at[k - 1, i], group, i == 0, 0, 0, w_here)
                if i == 0:
                    settle(k - 1)
            transform(k)

        @pl.when(jnp.logical_not(have))
        def _(k=k):
            out[:, k] = jnp.zeros((chans, share, half), F32)

    for k in range(far):
        last = (c + k < blocks) if k == far - 1 else (c + k == blocks - 1)

        @pl.when(last)
        def _(k=k):
            settle(k)

    @pl.when(gives)
    def _():
        for n in range(parts):
            far_result(n).wait_recv()
            a = pl.ds(n * at_once, at_once)
            out[a, far] = got[1, a]
        for i in range(win):
            for q in range(PIECES):
                up(i, q).wait_send()

    @pl.when(jnp.logical_not(gives))
    def _():
        out[:, far] = jnp.zeros((chans, share, half), F32)

    @pl.when(takes)
    def _():
        for n in range(parts):
            far_result(n).wait_send()

    for k in range(1, far):
        @pl.when((c >= 1) & (c + k - 1 < blocks))
        def _(k=k):
            for i in range(win):
                for q in range(PIECES):
                    down(k, i, q).wait_send()

    for d in range(1, win):
        for n in range(win):
            win_send(d, n).wait_send()


def body(blocks, win, spectra, dead_mask, partners):
    w_here, _, chans, bins = spectra.shape
    slots = partners.shape[1]
    share = chans // win
    half = LAGS // 2
    parts = chans * share // 256
    mask = jnp.broadcast_to(dead_mask.astype(F32)[:, None], (chans, LANES))
    dma = pltpu.SemaphoreType.DMA
    raw = pl.pallas_call(
        functools.partial(kernel, (blocks, win, slots)),
        out_shape=jax.ShapeDtypeStruct((chans, slots, share, half), F32),
        in_specs=[pl.BlockSpec(memory_space=pltpu.VMEM)] * 2,
        out_specs=pl.BlockSpec(memory_space=pltpu.VMEM),
        scratch_shapes=[
            pltpu.VMEM((win, win, w_here, 2 * share, bins), BF16),
            pltpu.VMEM((slots - 2, win, w_here, 2 * share, bins), BF16),
            pltpu.VMEM((win, win, w_here, 2 * share, bins), BF16),
            pltpu.VMEM((2, chans, share, half), F32),
            pltpu.VMEM((2, win * w_here, chans // ROWS_AT_ONCE, 4 * ROWS_AT_ONCE, bins), F32),
            pltpu.VMEM((w_here, 3 * share, bins), F32),
            pltpu.VMEM((2, 3, chans * share, bins), F32),
            pltpu.VMEM((bins, LAGS), BF16),
            pltpu.VMEM((bins, LAGS), BF16),
            pltpu.VMEM((bins, LAGS), BF16),
            pltpu.VMEM((bins, LAGS), BF16),
            pltpu.VMEM((slots, chans, share, half), F32),
            pltpu.VMEM((slots, chans, share, half), F32),
            dma((win - 1, win)),
            dma((win - 1, win)),
            dma((slots - 2, win, PIECES)),
            dma((slots - 2, win, PIECES)),
            dma((win, PIECES)),
            dma((win, PIECES)),
            dma((parts,)),
            dma((parts,)),
            dma((slots - 1,)),
            dma((slots - 1,)),
            dma((parts,)),
            dma((parts,)),
        ],
        compiler_params=pltpu.CompilerParams(
            collective_id=0, has_side_effects=True, vmem_limit_bytes=(44 if win == 2 else 60) * 2**20),
    )(spectra, mask)
    wanted = lax.dynamic_index_in_dim(partners, lax.axis_index("chan"), 0, keepdims=False)
    return jnp.where(wanted[None, :, None, None] >= 0, raw, 0.0)


def solution(mesh):
    placed = (P("win", None, ("groups", "chan"), "lag"), P(("groups", "chan")), P())
    return jax.shard_map(
        functools.partial(body, mesh.shape["chan"], mesh.shape["win"]),
        mesh=mesh,
        in_specs=placed,
        out_specs=P(("groups", "chan"), None, "win", "lag"),
        check_vma=False,
    )
```

```python
import functools
import math

import jax
import jax.numpy as jnp
from jax import lax
from jax.experimental import pallas as pl
from jax.experimental.pallas import tpu as pltpu
from jax.sharding import PartitionSpec as P

LAGS = 512
NSAMP = 15000
FLOW = 60
LANES = 128
ROWS_AT_ONCE = 4
PIECES = 4

water_level = 0.5

MESH = pl.DeviceIdType.MESH
F32 = jnp.float32
BF16 = jnp.bfloat16


def kernel(
    sizes, spectra, mask, out, own, ybuf, below, got, xf, yf, pacc, cos_hi, cos_lo, sin_hi, sin_lo,
    outgoing, incoming, xs, xr, zs, zr, us, ur, rs, rr, ls, lr, fs, fr,
):
    blocks, win, slots = sizes
    w_here, _, chans, bins = spectra.shape
    share = chans // win
    half = LAGS // 2
    c = lax.axis_index("chan")
    w = lax.axis_index("win")
    lag = lax.axis_index("lag")
    scale = (w_here * win * bins * 2) ** (-0.5)

    def lag_copy(k):
        return pltpu.make_async_remote_copy(
            outgoing.at[k], incoming.at[k], ls.at[k], lr.at[k],
            device_id={"lag": 1 - lag}, device_id_type=MESH)

    def win_send(d, n):
        peer = lax.rem(w + d, win)
        g = lax.rem(peer + n, win)
        return pltpu.make_async_remote_copy(
            own.at[w, g], own.at[w, g], xs.at[d - 1, n], xr.at[d - 1, n],
            device_id={"win": peer}, device_id_type=MESH)

    def win_arrival(d, n):
        source = lax.rem(w + win - d, win)
        g = lax.rem(w + n, win)
        return pltpu.make_async_remote_copy(
            own.at[source, g], own.at[source, g], xs.at[d - 1, n], xr.at[d - 1, n],
            device_id={"win": source}, device_id_type=MESH)

    piece = w_here // PIECES

    def down(k, i, q):
        g = lax.rem(w + i, win)
        src = own.at[g, w] if k == 1 else ybuf.at[k - 2, i]
        part = pl.ds(q * piece, piece)
        return pltpu.make_async_remote_copy(
            src.at[part], ybuf.at[k - 1, i, part], zs.at[k - 1, i, q], zr.at[k - 1, i, q],
            device_id={"chan": c - 1}, device_id_type=MESH)

    far = slots - 1
    gives = c + far < blocks
    takes = (c >= 1) & (c - 1 + far < blocks)
    at_once = 256 // share
    parts = chans // at_once

    def up(i, q):
        g = lax.rem(w + i, win)
        part = pl.ds(q * piece, piece)
        return pltpu.make_async_remote_copy(
            own.at[g, :, part], below.at[g, :, part], us.at[i, q], ur.at[i, q],
            device_id={"chan": c + 1}, device_id_type=MESH)

    def far_lag(n):
        a = pl.ds(n * at_once, at_once)
        return pltpu.make_async_remote_copy(
            outgoing.at[far, a], incoming.at[far, a], fs.at[n], fr.at[n],
            device_id={"lag": 1 - lag}, device_id_type=MESH)

    def far_result(n):
        a = pl.ds(n * at_once, at_once)
        return pltpu.make_async_remote_copy(
            got.at[0, a], got.at[1, a], rs.at[n], rr.at[n],
            device_id={"chan": c - 1}, device_id_type=MESH)

    def send_up(i):
        @pl.when(gives)
        def _():
            for q in range(PIECES):
                up(i, q).start()

    def send_down(k, i):
        @pl.when((c >= 1) & (c + k - 1 < blocks))
        def _():
            for q in range(PIECES):
                down(k, i, q).start()

    barrier = pltpu.get_barrier_semaphore()
    pl.semaphore_signal(barrier, inc=1, device_id={"lag": 1 - lag}, device_id_type=MESH)
    for d in range(1, win):
        pl.semaphore_signal(barrier, inc=1, device_id={"win": lax.rem(w + d, win)}, device_id_type=MESH)

    @pl.when(c >= 1)
    def _():
        pl.semaphore_signal(barrier, inc=1, device_id={"chan": c - 1}, device_id_type=MESH)

    @pl.when(c + 1 < blocks)
    def _():
        pl.semaphore_signal(barrier, inc=1, device_id={"chan": c + 1}, device_id_type=MESH)

    def whiten(v, carry):
        re = spectra[v, 0].astype(F32)
        im = spectra[v, 1].astype(F32)
        amplitude = jnp.sqrt(re * re + im * im)
        factor = mask[:, 0:1] / jnp.maximum(amplitude, water_level)
        re = re * factor
        im = im * factor
        for g in range(win):
            rows = slice(g * share, (g + 1) * share)
            own[w, g, v] = jnp.concatenate([re[rows], im[rows]], axis=0).astype(BF16)
        return carry

    lax.fori_loop(0, w_here, whiten, 0)

    edges = (c >= 1).astype(jnp.int32) + (c + 1 < blocks).astype(jnp.int32)
    pl.semaphore_wait(barrier, win + edges)

    for d in range(1, win):
        win_send(d, 0).start()
    send_down(1, 0)
    send_up(0)
    for d in range(1, win):
        for n in range(1, win):
            win_send(d, n).start()

    def widen(blockref, group, which, start, count):
        def step(v, carry):
            for g in range(win):
                value = blockref[group, g, v].astype(F32)
                re, im = value[:share], value[share:]
                at = group * w_here + v
                for b in range(share // ROWS_AT_ONCE):
                    to = g * share // ROWS_AT_ONCE + b
                    rows = slice(b * ROWS_AT_ONCE, (b + 1) * ROWS_AT_ONCE)
                    for t, part in enumerate((re, im, re + im)):
                        xf[which, at, to, t * ROWS_AT_ONCE:(t + 1) * ROWS_AT_ONCE] = part[rows]
            return carry

        lax.fori_loop(start, start + count, step, 0)

    def stack_step(src, group, fresh, which, start, count):
        def convert(v, carry):
            value = src[start + v].astype(F32)
            re, im = value[:share], value[share:]
            yf[v, 0:share] = re
            yf[v, share:2 * share] = im
            yf[v, 2 * share:3 * share] = re - im
            return carry

        lax.fori_loop(0, count, convert, 0)
        tiles = bins // LANES

        def rows(n, carry):
            b = n // tiles
            a0 = b * ROWS_AT_ONCE
            col = pl.ds(pl.multiple_of(lax.rem(n, tiles) * LANES, LANES), LANES)
            total = [[None] * 3 for _ in range(ROWS_AT_ONCE)]
            for aa in range(ROWS_AT_ONCE):
                for t in range(3):
                    if fresh is True:
                        total[aa][t] = jnp.zeros((share, LANES), F32)
                    else:
                        total[aa][t] = pacc[which, t, pl.ds(pl.multiple_of((a0 + aa) * share, share), share), col]
                        if fresh is not False:
                            total[aa][t] = jnp.where(fresh, 0.0, total[aa][t])
            for v in range(count):
                y = [yf[v, t * share:(t + 1) * share, col] for t in range(3)]
                for aa in range(ROWS_AT_ONCE):
                    for t in range(3):
                        line = t * ROWS_AT_ONCE + aa
                        x = xf[which % 2, group * w_here + start + v, b, line:line + 1, col]
                        total[aa][t] = total[aa][t] + x * y[t]
            for aa in range(ROWS_AT_ONCE):
                for t in range(3):
                    pacc[which, t, pl.ds(pl.multiple_of((a0 + aa) * share, share), share), col] = total[aa][t]
            return carry

        lax.fori_loop(0, (chans // ROWS_AT_ONCE) * tiles, rows, 0)

    def rows_out(n, which):
            r = pl.ds(pl.multiple_of(n * 256, 256), 256)
            p1, p2, p3 = pacc[which, 0, r], pacc[which, 1, r], pacc[which, 2, r]
            re = p1 + p2
            im = p3 - p1 + p2
            re_hi = re.astype(BF16)
            re_lo = (re - re_hi.astype(F32)).astype(BF16)
            im_hi = im.astype(BF16)
            im_lo = (im - im_hi.astype(F32)).astype(BF16)
            dot = functools.partial(jnp.dot, preferred_element_type=F32)
            total = dot(re_hi, cos_hi[...]) + dot(im_hi, sin_hi[...])
            total += dot(re_lo, cos_hi[...]) + dot(im_lo, sin_hi[...])
            total += dot(re_hi, cos_lo[...]) + dot(im_hi, sin_lo[...])
            here = total[:, :half].reshape(at_once, share, half)
            there = total[:, half:].reshape(at_once, share, half)
            return here, there

    def transform(k, which=0):
        def part(n, carry):
            a = pl.ds(n * at_once, at_once)
            out[a, k], outgoing[k, a] = rows_out(n, which)
            return carry

        lax.fori_loop(0, parts, part, 0)
        lag_copy(k).start()

    def settle(k):
        lag_copy(k).wait()

        def add(n, carry):
            a = pl.ds(n * 4, 4)
            out[a, k] = (out[a, k] + incoming[k, a]) * scale
            return carry

        lax.fori_loop(0, chans // 4, add, 0)

    def phases(n, carry):
        r = pl.ds(pl.multiple_of(n * 16, 16), 16)
        bin_no = FLOW + lag * bins + n * 16 + lax.broadcasted_iota(jnp.int32, (16, LAGS), 0)
        place = lax.broadcasted_iota(jnp.int32, (16, LAGS), 1) + lag * half
        place = jnp.where(place >= LAGS, place - LAGS, place) - LAGS // 2
        product = bin_no * place
        laps = jnp.floor(product.astype(F32) * (1.0 / NSAMP)).astype(jnp.int32)
        turns = product - laps * NSAMP
        turns = jnp.where(turns < 0, turns + NSAMP, turns)
        turns = jnp.where(turns >= NSAMP, turns - NSAMP, turns)
        angle = turns.astype(F32) * (2.0 * math.pi / NSAMP)
        cos, sin = jnp.cos(angle), -jnp.sin(angle)
        hi = cos.astype(BF16)
        cos_hi[r] = hi
        cos_lo[r] = (cos - hi.astype(F32)).astype(BF16)
        hi = sin.astype(BF16)
        sin_hi[r] = hi
        sin_lo[r] = (sin - hi.astype(F32)).astype(BF16)
        return carry

    lax.fori_loop(0, bins // 16, phases, 0)

    def far_finish():
        for n in range(parts):
            a = pl.ds(n * at_once, at_once)
            got[0, a], outgoing[far, a] = rows_out(n, 1)
            far_lag(n).start()
        for n in range(parts):
            a = pl.ds(n * at_once, at_once)
            far_lag(n).wait()
            got[0, a] = (got[0, a] + incoming[far, a]) * scale
            far_result(n).start()

    def take(k, i):
        @pl.when(c + k < blocks)
        def _():
            for q in range(PIECES):
                down(k, i, q).wait_recv()
        send_down(k + 1, i)

    widen(own, w, 0, 0, w_here)
    stack_step(own.at[w, w], w, True, 0, 0, w_here)
    for i in range(1, win):
        win_arrival(win - i, 0).wait_recv()
        send_down(1, i)
    take(1, 0)

    @pl.when(c + 1 < blocks)
    def _():
        stack_step(ybuf.at[0, 0], w, True, 2, 0, w_here)

    for i in range(1, win):
        for n in range(1, win):
            win_arrival(win - i, n).wait_recv()
        send_up(i)
        group = lax.rem(w + i, win)
        widen(own, group, 0, 0, w_here)
        stack_step(own.at[group, w], group, False, 0, 0, w_here)
        take(1, i)
    transform(0)

    def far_step(k, i, q):
        group = lax.rem(w + i, win)
        start = q * piece
        up(i, q).wait_recv()
        widen(below, group, 1, start, piece)
        stack_step(ybuf.at[k - 1, i], group, (q == 0) if i == 0 else False, 1, start, piece)

    for k in range(1, far):
        have = c + k < blocks

        @pl.when(have)
        def _(k=k):
            for i in range(win):
                group = lax.rem(w + i, win)
                if k + 1 == far:
                    def arrive(q, carry):
                        down(k, i, q).wait_recv()

                        @pl.when(takes)
                        def _():
                            far_step(k, i, q)
                        return carry

                    lax.fori_loop(0, PIECES, arrive, 0)
                    if i == win - 1:
                        pl.when(takes)(far_finish)
                elif k > 1:
                    take(k, i)
                if k > 1 or i > 0:
                    stack_step(ybuf.at[k - 1, i], group, i == 0, 2 if k == 1 else 0, 0, w_here)
                if i == 0 and k > 1:
                    settle(k - 1)
            transform(k, 2 if k == 1 else 0)
            if k == 1:
                settle(0)

        @pl.when(jnp.logical_not(have))
        def _(k=k):
            out[:, k] = jnp.zeros((chans, share, half), F32)

    for k in range(far):
        last = (c + k < blocks) if k == far - 1 else (c + k == blocks - 1)

        @pl.when(last)
        def _(k=k):
            settle(k)

    @pl.when(gives)
    def _():
        for n in range(parts):
            far_result(n).wait_recv()
            a = pl.ds(n * at_once, at_once)
            out[a, far] = got[1, a]
        for i in range(win):
            for q in range(PIECES):
                up(i, q).wait_send()

    @pl.when(jnp.logical_not(gives))
    def _():
        out[:, far] = jnp.zeros((chans, share, half), F32)

    @pl.when(takes)
    def _():
        for n in range(parts):
            far_result(n).wait_send()

    for k in range(1, far):
        @pl.when((c >= 1) & (c + k - 1 < blocks))
        def _(k=k):
            for i in range(win):
                for q in range(PIECES):
                    down(k, i, q).wait_send()

    for d in range(1, win):
        for n in range(win):
            win_send(d, n).wait_send()


def body(blocks, win, spectra, dead_mask, partners):
    w_here, _, chans, bins = spectra.shape
    slots = partners.shape[1]
    share = chans // win
    half = LAGS // 2
    parts = chans * share // 256
    mask = jnp.broadcast_to(dead_mask.astype(F32)[:, None], (chans, LANES))
    dma = pltpu.SemaphoreType.DMA
    raw = pl.pallas_call(
        functools.partial(kernel, (blocks, win, slots)),
        out_shape=jax.ShapeDtypeStruct((chans, slots, share, half), F32),
        in_specs=[pl.BlockSpec(memory_space=pltpu.VMEM)] * 2,
        out_specs=pl.BlockSpec(memory_space=pltpu.VMEM),
        scratch_shapes=[
            pltpu.VMEM((win, win, w_here, 2 * share, bins), BF16),
            pltpu.VMEM((slots - 2, win, w_here, 2 * share, bins), BF16),
            pltpu.VMEM((win, win, w_here, 2 * share, bins), BF16),
            pltpu.VMEM((2, chans, share, half), F32),
            pltpu.VMEM((2, win * w_here, chans // ROWS_AT_ONCE, 4 * ROWS_AT_ONCE, bins), F32),
            pltpu.VMEM((w_here, 3 * share, bins), F32),
            pltpu.VMEM((3, 3, chans * share, bins), F32),
            pltpu.VMEM((bins, LAGS), BF16),
            pltpu.VMEM((bins, LAGS), BF16),
            pltpu.VMEM((bins, LAGS), BF16),
            pltpu.VMEM((bins, LAGS), BF16),
            pltpu.VMEM((slots, chans, share, half), F32),
            pltpu.VMEM((slots, chans, share, half), F32),
            dma((win - 1, win)),
            dma((win - 1, win)),
            dma((slots - 2, win, PIECES)),
            dma((slots - 2, win, PIECES)),
            dma((win, PIECES)),
            dma((win, PIECES)),
            dma((parts,)),
            dma((parts,)),
            dma((slots - 1,)),
            dma((slots - 1,)),
            dma((parts,)),
            dma((parts,)),
        ],
        compiler_params=pltpu.CompilerParams(
            collective_id=0, has_side_effects=True, vmem_limit_bytes=(47 if win == 2 else 60) * 2**20),
    )(spectra, mask)
    wanted = lax.dynamic_index_in_dim(partners, lax.axis_index("chan"), 0, keepdims=False)
    return jnp.where(wanted[None, :, None, None] >= 0, raw, 0.0)


def solution(mesh):
    placed = (P("win", None, ("groups", "chan"), "lag"), P(("groups", "chan")), P())
    return jax.shard_map(
        functools.partial(body, mesh.shape["chan"], mesh.shape["win"]),
        mesh=mesh,
        in_specs=placed,
        out_specs=P(("groups", "chan"), None, "win", "lag"),
        check_vma=False,
    )
```
